512 devices in a mesh: frame: 32 (over z, y_lo), head: 16 (over y_hi, x, core).
Axes of the slice: x: 4, y: 4 (y_hi: 2, y_lo: 2; y = y_hi * 2 + y_lo), z: 16, core: 2. Of those that a mesh axis runs over, the one named last changes fastest.
Arguments:
- latents: bfloat16 [32, 512, 1152], P('frame', 'head'), may hold values from -9 to 9
- spatial_qkv: bfloat16 [3, 1152, 1152], P(None, 'head'), may hold values from -0.5 to 0.5
- spatial_out: bfloat16 [1152, 1152], P('head'), may hold values from -0.375 to 0.375
- temporal_qkv: bfloat16 [3, 1152, 1152], P(None, 'head'), may hold values from -0.5 to 0.5
- temporal_out: bfloat16 [1152, 1152], P('head'), may hold values from -0.375 to 0.375
- modulation: float32 [4, 1152], replicated, may hold values from -2.5 to 2.5
- gates: float32 [2, 1152], replicated, may hold values from 0.5 to 2
- out_bias: float32 [2, 1152], replicated, may hold values from -2.5 to 2.5
Outputs:
- mixed: bfloat16 [32, 512, 1152], P('frame', 'head')
The draws below stay inside these ranges and needn't reach their ends.
All inputs are finite; a program needn't handle non-finite values.
Results may differ from the reference program's by a relative error of at most 0.015.
Values may be sent and summed in bfloat16 or wider, within the bound.
A program may use at most 64 MiB of HBM per device.

```python
import jax
import jax.numpy as jnp
from jax import lax

D = 1152
HEADS = 16
HD = 72
FRAMES = 32
POSITIONS = 512


def draw_latents(key, part):
    key = jax.random.fold_in(key, 11)
    first = jax.random.fold_in(key, 0)
    noise = jax.random.normal(first, (FRAMES, POSITIONS, D), jnp.float32)
    return jnp.clip(noise * 0.5, -3.0, 3.0).astype(jnp.bfloat16)


def projection_draw(key):
    first = jax.random.fold_in(key, 0)
    scales = jnp.array([1.1, 1.1, 1.0], jnp.float32).reshape(3, 1, 1) * D ** (-0.5)
    noise = jnp.clip(jax.random.normal(first, (3, D, D), jnp.float32), -4.0, 4.0)
    return jnp.clip(noise * scales, -0.5, 0.5).astype(jnp.bfloat16)


def draw_spatial_qkv(key, part):
    key = jax.random.fold_in(key, 23)
    return projection_draw(key)


def draw_temporal_qkv(key, part):
    key = jax.random.fold_in(key, 37)
    return projection_draw(key)


def level_of(stream_key, extent, shards, low, largest):
    level, own = 1.0, jax.random.fold_in(stream_key, 6)
    for position, blocks in shards:
        draws = jnp.exp(jax.random.uniform(jax.random.fold_in(own, position), (blocks,), jnp.float32, low / len(shards), largest / len(shards)))
        level = level * jnp.repeat(draws, extent[position] // blocks).reshape([-1 if axis == position else 1 for axis in range(len(extent))])
    return level


def bell_draw(own_key, dims, width, bound, cuts=(), held_as=jnp.bfloat16):
    values = width * jax.random.normal(own_key, dims, jnp.float32)
    if cuts:
        values = values * level_of(own_key, dims, cuts, -0.22, 0.18)
    return jnp.clip(values, -bound, bound).astype(held_as)


def setup_inputs(seed: int = 0) -> dict:
    streams_of = jax.random.split(jax.random.key(seed), 9)
    latents = draw_latents(jax.random.fold_in(streams_of[8], 71), 0)
    spatial_qkv = draw_spatial_qkv(jax.random.fold_in(streams_of[8], 71), 0)
    spatial_out = bell_draw(streams_of[2], (D, D), (D // 4) ** -0.5, 0.375, ((0, 16),))
    temporal_qkv = draw_temporal_qkv(jax.random.fold_in(streams_of[8], 71), 0)
    temporal_out = bell_draw(streams_of[4], (D, D), (D // 4) ** -0.5, 0.375, ((0, 16),))
    modulation = bell_draw(streams_of[5], (4, D), 0.4, 2.5, (), jnp.float32)
    gates = jnp.clip(jax.random.uniform(streams_of[6], (2, D), jnp.float32, 0.5, 2.0), 0.5, 2.0)
    out_bias = bell_draw(streams_of[7], (2, D), 0.3, 2.5, (), jnp.float32)
    return dict(latents=latents, spatial_qkv=spatial_qkv, spatial_out=spatial_out, temporal_qkv=temporal_qkv, temporal_out=temporal_out, modulation=modulation, gates=gates, out_bias=out_bias)


def normalize(tensor, shift_row, scale_row):
    values = tensor.astype(jnp.float32)
    centre = lax.optimization_barrier(jnp.mean(values, axis=-1, keepdims=True))
    offsets = values - centre
    spread = lax.optimization_barrier(jnp.mean(offsets * offsets, axis=-1, keepdims=True))
    return (offsets * lax.rsqrt(spread + 1e-06) * (1.0 + scale_row) + shift_row).astype(jnp.bfloat16)

def project_all(inputs, weight):
    flat = inputs.reshape(-1, D)
    results = []
    for member in range(3):
        product = jnp.dot(flat, weight[member].T, preferred_element_type=jnp.float32)
        results.append(product.astype(jnp.bfloat16).reshape(inputs.shape))
    return results

def spatial_attention(queries, key_rows, values):

    def one_frame(triple):
        query_f = triple[0].astype(jnp.float32).reshape(POSITIONS, HEADS, HD)
        key_f = triple[1].astype(jnp.float32).reshape(POSITIONS, HEADS, HD)
        value_f = triple[2].astype(jnp.float32).reshape(POSITIONS, HEADS, HD)
        scores = jnp.einsum('qhd,khd->hqk', query_f, key_f) * HD ** (-0.5)
        weights = jax.nn.softmax(scores, axis=-1).astype(jnp.bfloat16)
        summed = jnp.einsum('hqk,khd->qhd', weights.astype(jnp.float32), value_f)
        return summed.astype(jnp.bfloat16).reshape(POSITIONS, D)
    return lax.map(one_frame, (queries, key_rows, values))

def temporal_attention(queries, key_rows, values):
    query_f = queries.astype(jnp.float32).reshape(FRAMES, POSITIONS, HEADS, HD)
    key_f = key_rows.astype(jnp.float32).reshape(FRAMES, POSITIONS, HEADS, HD)
    value_f = values.astype(jnp.float32).reshape(FRAMES, POSITIONS, HEADS, HD)
    scores = jnp.einsum('qshd,kshd->shqk', query_f, key_f) * HD ** (-0.5)
    weights = jax.nn.softmax(scores, axis=-1).astype(jnp.bfloat16)
    summed = jnp.einsum('shqk,kshd->qshd', weights.astype(jnp.float32), value_f)
    return summed.astype(jnp.bfloat16).reshape(FRAMES, POSITIONS, D)

def out_branch(heads_out, weight, bias_row, gate_row, residual):
    product = jnp.dot(heads_out.reshape(-1, D), weight, preferred_element_type=jnp.float32)
    product = product.reshape(residual.shape)
    return (residual.astype(jnp.float32) + gate_row * (product + bias_row)).astype(jnp.bfloat16)

def reference(latents, spatial_qkv, spatial_out, temporal_qkv, temporal_out, modulation, gates, out_bias):
    spatial_input = normalize(latents, modulation[0], modulation[1])
    queries, key_rows, values = project_all(spatial_input, spatial_qkv)
    spatial_heads = spatial_attention(queries, key_rows, values)
    frame_section = out_branch(spatial_heads, spatial_out, out_bias[0], gates[0], latents)
    temporal_input = normalize(frame_section, modulation[2], modulation[3])
    queries, key_rows, values = project_all(temporal_input, temporal_qkv)
    temporal_heads = temporal_attention(queries, key_rows, values)
    return out_branch(temporal_heads, temporal_out, out_bias[1], gates[1], frame_section)
```

```python
import functools

import jax
import jax.numpy as jnp
from jax import lax
from jax.experimental import pallas as pl
from jax.experimental.pallas import tpu as pltpu
from jax.sharding import PartitionSpec as P

HD = 72
PAD = 128
WROWS = 80
D = 1152
TOK = 32
HEADS = 16
SCALE2 = HD**-0.5 * 1.4426950408889634
MESH = pl.DeviceIdType.MESH


def normalize(values, shift_row, scale_row):
    centre = jnp.mean(values, axis=-1, keepdims=True)
    offsets = values - centre
    spread = jnp.mean(offsets * offsets, axis=-1, keepdims=True)
    return (offsets * lax.rsqrt(spread + 1e-6) * (1.0 + scale_row) + shift_row).astype(jnp.bfloat16)


def places():
    frame, head = lax.axis_index("frame"), lax.axis_index("head")
    return frame // 2, frame % 2, head // 8, (head // 2) % 4, head % 2


def group_place(half):
    z, yl, yh, x, c = places()
    zg = c * 8 + half * 4 + x
    delta = (z - zg + 16) % 16
    line = ((1 - yl) * delta + yl * (16 - delta)) % 8
    core = (yl + zg // 8 + 1) % 2
    return (zg * 2 + yh, (line // 4) * 8 + (line % 4) * 2 + core), delta // 8


def frame_place(slot):
    z, yl, yh, x, c = places()
    ylf = (c + z // 8 + 1) % 2
    line = yh * 4 + x
    delta = ((1 - ylf) * line + ylf * (8 - line)) % 8 + 8 * slot
    zf = (z + delta) % 16
    return (zf * 2 + ylf, yl * 8 + (z % 4) * 2 + z // 8), (z // 4) % 2


def remote(src, dst, send, recv, device):
    return pltpu.make_async_remote_copy(
        src_ref=src, dst_ref=dst, send_sem=send, recv_sem=recv, device_id=device, device_id_type=MESH
    )


def kernel(
    lat_ref, sqkv_ref, so_ref, tqkv_ref, to_ref, mod_ref, gate_ref, bias_ref,
    out_ref,
    x0, x1, wm0, wm1, wb0, wb1, o0, o1, h0, h1, y0, y1, p0, p1,
    ag_s, ag_r, sib_s, sib_r, w_s, w_r, ws_s, ws_r, a_s, a_r, p_s, p_r,
):
    frame, head = lax.axis_index("frame"), lax.axis_index("head")
    _, _, yh, x, c = places()
    sibling = (frame, yh * 8 + x * 2 + 1 - c)
    pending = []

    def chip(k, sign):
        return ((yh + k // 4) % 2) * 8 + ((x + sign * (k % 4) + 4) % 4) * 2 + c

    barrier = pltpu.get_barrier_semaphore()
    for d in range(1, HEADS):
        pl.semaphore_signal(barrier, inc=1, device_id=(frame, (head + d) % HEADS), device_id_type=MESH)
    for i in range(2):
        pl.semaphore_signal(barrier, inc=1, device_id=group_place(i)[0], device_id_type=MESH)
        pl.semaphore_signal(barrier, inc=1, device_id=frame_place(i)[0], device_id_type=MESH)

    own_rows = pl.ds(pl.multiple_of(head * TOK, TOK), TOK)
    own_w = pl.ds(pl.multiple_of(head * PAD, PAD), WROWS)
    latents = lat_ref[0].astype(jnp.float32)
    x0[own_rows, :] = normalize(latents, mod_ref[0:1, :], mod_ref[1:2, :])
    for wm, qkv_ref in ((wm0, sqkv_ref), (wm1, tqkv_ref)):
        for m in range(3):
            wm[m * PAD + 64 : (m + 1) * PAD, :] = jnp.zeros((64, D), jnp.bfloat16)
            wm[m * PAD : m * PAD + HD, :] = qkv_ref[m]
    for wb, wo_ref in ((wb0, so_ref), (wb1, to_ref)):
        for k in range(HEADS):
            wb[k * PAD + WROWS : (k + 1) * PAD, :] = jnp.zeros((PAD - WROWS, D), jnp.bfloat16)
        wb[own_w, :] = jnp.concatenate([wo_ref[...], jnp.zeros((WROWS - HD, D), jnp.bfloat16)], axis=0)
    pl.semaphore_wait(barrier, HEADS - 1 + 4)

    ORDER = (2, 6, 5, 7, 4, 1, 3)

    def start(copy):
        copy.start()
        pending.append(copy)

    def send_tokens(st, xb):
        start(remote(xb.at[own_rows], xb.at[own_rows], sib_s.at[st, 0], sib_r.at[st, 0], sibling))
        for k in ORDER:
            start(remote(xb.at[own_rows], xb.at[own_rows], ag_s.at[st, k], ag_r.at[st, k], (frame, chip(k, 1))))

    def gather_tokens(st, xb):
        for k in ORDER[::-1]:
            rows = pl.ds(pl.multiple_of(chip(k, -1) * TOK, TOK), TOK)
            remote(xb.at[rows], xb.at[rows], ag_s.at[st, k], ag_r.at[st, k], sibling).wait_recv()
            start(remote(xb.at[rows], xb.at[rows], sib_s.at[st, k], sib_r.at[st, k], sibling))
        for k in (0,) + ORDER[::-1]:
            rows = pl.ds(pl.multiple_of((chip(k, -1) + 1 - 2 * c) * TOK, TOK), TOK)
            remote(xb.at[rows], xb.at[rows], sib_s.at[st, k], sib_r.at[st, k], sibling).wait_recv()

    def send_weight(st, wb):
        start(remote(wb.at[own_w], wb.at[own_w], ws_s.at[st, 0], ws_r.at[st, 0], sibling))
        for k in ORDER:
            start(remote(wb.at[own_w], wb.at[own_w], w_s.at[st, k], w_r.at[st, k], (frame, chip(k, 1))))

    def forward_weight(st, wb):
        for k in ORDER[::-1]:
            rows = pl.ds(pl.multiple_of(chip(k, -1) * PAD, PAD), WROWS)
            remote(wb.at[rows], wb.at[rows], w_s.at[st, k], w_r.at[st, k], sibling).wait_recv()
            start(remote(wb.at[rows], wb.at[rows], ws_s.at[st, k], ws_r.at[st, k], sibling))

    def wait_weight(st, wb):
        for k in (0,) + ORDER[::-1]:
            rows = pl.ds(pl.multiple_of((chip(k, -1) + 1 - 2 * c) * PAD, PAD), WROWS)
            remote(wb.at[rows], wb.at[rows], ws_s.at[st, k], ws_r.at[st, k], sibling).wait_recv()

    def attend(xb, wm, ob, same_position):
        proj = lax.dot_general(
            xb[...], wm[...], (((1,), (1,)), ((), ())), preferred_element_type=jnp.float32
        )
        total = HEADS * TOK
        queries = proj[:, :PAD].astype(jnp.bfloat16)
        keys = proj[:, PAD : 2 * PAD].astype(jnp.bfloat16)
        lane = lax.broadcasted_iota(jnp.int32, (total, PAD), 1)
        values = jnp.where(lane == HD, 1.0, proj[:, 2 * PAD :]).astype(jnp.bfloat16)
        block = 128
        for i in range(total // block):
            scores = lax.dot_general(
                queries[i * block : (i + 1) * block], keys, (((1,), (1,)), ((), ())),
                preferred_element_type=jnp.float32,
            )
            if same_position:
                row = lax.broadcasted_iota(jnp.int32, (block, total), 0)
                col = lax.broadcasted_iota(jnp.int32, (block, total), 1)
                scores = jnp.where(((row - col) & 15) == 0, scores, -1e30)
            largest = jnp.max(scores, axis=-1, keepdims=True)
            weights = jnp.exp2((scores - largest) * SCALE2).astype(jnp.bfloat16)
            summed = jnp.dot(weights, values, preferred_element_type=jnp.float32)
            ob[i * block : (i + 1) * block, :] = (summed / summed[:, HD : HD + 1]).astype(jnp.bfloat16)

    def send_heads(st, ob, hb):
        hb[pl.ds(head, 1)] = ob[own_rows, :].reshape(1, TOK, PAD)
        for d in range(1, HEADS):
            other = (head + d) % HEADS
            rows = pl.ds(pl.multiple_of(other * TOK, TOK), TOK)
            start(remote(ob.at[rows], hb.at[head], a_s.at[st, d], a_r.at[st, d], (frame, other)))

    def project(st, hb, wb):
        for d in range(1, HEADS):
            other = (head + HEADS - d) % HEADS
            remote(hb.at[other], hb.at[other], a_s.at[st, d], a_r.at[st, d], sibling).wait_recv()
        flat = jnp.concatenate([hb[k] for k in range(HEADS)], axis=1)
        branch = jnp.dot(flat, wb[...], preferred_element_type=jnp.float32)
        return gate_ref[st : st + 1, :] * (branch + bias_ref[st : st + 1, :])

    send_tokens(0, x0)
    gather_tokens(0, x0)
    send_weight(0, wb0)
    attend(x0, wm0, o0, False)
    send_heads(0, o0, h0)
    forward_weight(0, wb0)
    wait_weight(0, wb0)
    y0[...] = (latents + project(0, h0, wb0)).astype(jnp.bfloat16)

    for i in range(2):
        device, slot = group_place(i)
        start(remote(y0.at[i * 16 : i * 16 + 16], p0.at[slot], p_s.at[0, i], p_r.at[0, slot], device))
    send_weight(1, wb1)
    for i in range(2):
        remote(p0.at[i], p0.at[i], p_s.at[0, i], p_r.at[0, i], sibling).wait_recv()

    section = p0[...].reshape(TOK, D).astype(jnp.float32)
    x1[own_rows, :] = normalize(section, mod_ref[2:3, :], mod_ref[3:4, :])
    send_tokens(1, x1)
    gather_tokens(1, x1)
    attend(x1, wm1, o1, True)
    send_heads(1, o1, h1)
    forward_weight(1, wb1)
    wait_weight(1, wb1)
    y1[...] = (section + project(1, h1, wb1)).astype(jnp.bfloat16)

    for i in range(2):
        device, half = frame_place(i)
        start(remote(y1.at[i * 16 : i * 16 + 16], p1.at[half], p_s.at[1, i], p_r.at[1, half], device))
    for i in range(2):
        remote(p1.at[i], p1.at[i], p_s.at[1, i], p_r.at[1, i], sibling).wait_recv()
    out_ref[...] = p1[...].reshape(1, TOK, D)
    for copy in pending:
        copy.wait_send()


def local(latents, spatial_qkv, spatial_out, temporal_qkv, temporal_out, modulation, gates, out_bias):
    bf16, vmem, dma = jnp.bfloat16, pltpu.VMEM, pltpu.SemaphoreType.DMA
    total = HEADS * TOK
    return pl.pallas_call(
        kernel,
        out_shape=jax.ShapeDtypeStruct(latents.shape, bf16),
        in_specs=[pl.BlockSpec(memory_space=pltpu.VMEM)] * 8,
        out_specs=pl.BlockSpec(memory_space=pltpu.VMEM),
        scratch_shapes=[
            vmem((total, D), bf16), vmem((total, D), bf16),
            vmem((3 * PAD, D), bf16), vmem((3 * PAD, D), bf16),
            vmem((HEADS * PAD, D), bf16), vmem((HEADS * PAD, D), bf16),
            vmem((total, PAD), bf16), vmem((total, PAD), bf16),
            vmem((HEADS, TOK, PAD), bf16), vmem((HEADS, TOK, PAD), bf16),
            vmem((TOK, D), bf16), vmem((TOK, D), bf16),
            vmem((2, TOK // 2, D), bf16), vmem((2, TOK // 2, D), bf16),
            dma((2, 8)), dma((2, 8)), dma((2, 8)), dma((2, 8)),
            dma((2, 8)), dma((2, 8)), dma((2, 8)), dma((2, 8)),
            dma((2, 16)), dma((2, 16)), dma((2, 2)), dma((2, 2)),
        ],
        compiler_params=pltpu.CompilerParams(
            collective_id=0, has_side_effects=True, vmem_limit_bytes=48 << 20
        ),
        name="block_pair",
    )(latents, spatial_qkv, spatial_out, temporal_qkv, temporal_out, modulation, gates, out_bias)


def solution(mesh):
    return jax.shard_map(
        local,
        mesh=mesh,
        in_specs=(
            P("frame", "head", None),
            P(None, "head", None),
            P("head", None),
            P(None, "head", None),
            P("head", None),
            P(),
            P(),
            P(),
        ),
        out_specs=P("frame", "head", None),
        check_vma=False,
    )
```

```python
import jax
import jax.numpy as jnp
from jax import lax
from jax.experimental import pallas as pl
from jax.experimental.pallas import tpu as pltpu
from jax.sharding import PartitionSpec as P

HD = 72
PAD = 128
D = 1152
TOK = 32
TOTAL = 512
NEAR = (1, 3, 4, 2, 5, 7, 6)
FAR = NEAR[::-1]
SCALE2 = HD**-0.5 * 1.4426950408889634
MESH = pl.DeviceIdType.MESH


def normalize(values, shift_row, scale_row):
    centre = jnp.mean(values, axis=-1, keepdims=True)
    offsets = values - centre
    spread = jnp.mean(offsets * offsets, axis=-1, keepdims=True)
    return (offsets * lax.rsqrt(spread + 1e-6) * (1.0 + scale_row) + shift_row).astype(jnp.bfloat16)


def places():
    frame, head = lax.axis_index("frame"), lax.axis_index("head")
    return frame // 2, frame % 2, head // 8, (head // 2) % 4, head % 2


def group_place(half):
    z, yl, yh, x, c = places()
    zg = c * 8 + half * 4 + x
    delta = (z - zg + 16) % 16
    line = ((1 - yl) * delta + yl * (16 - delta)) % 8
    core = (yl + zg // 8 + 1) % 2
    return (zg * 2 + yh, (line // 4) * 8 + (line % 4) * 2 + core), delta // 8


def frame_place(slot):
    z, yl, yh, x, c = places()
    ylf = (c + z // 8 + 1) % 2
    line = yh * 4 + x
    delta = ((1 - ylf) * line + ylf * (8 - line)) % 8 + 8 * slot
    zf = (z + delta) % 16
    return (zf * 2 + ylf, yl * 8 + (z % 4) * 2 + z // 8), (z // 4) % 2


def remote(src, dst, send, recv, device):
    return pltpu.make_async_remote_copy(
        src_ref=src, dst_ref=dst, send_sem=send, recv_sem=recv, device_id=device, device_id_type=MESH
    )


def kernel(
    lat_hbm, sqkv_hbm, so_hbm, tqkv_hbm, to_hbm, mod_hbm, gate_hbm, bias_hbm,
    out_ref,
    lat_ref, qkv0, qkv1, wo0, wo1, mod_ref, gate_ref, bias_ref,
    x0, x1, wm0, wm1, wp0, wp1, o0, o1, u0, u1, v0, v1, t0, t1, r0, r1, acc, y0, y1, p0, p1,
    in_s, ag_s, ag_r, sib_s, sib_r, u_s, u_r, t_s, t_r, p_s, p_r,
):
    frame = lax.axis_index("frame")
    z, yl, yh, x, c = places()
    head = yh * 8 + x * 2 + c
    sibling = (frame, yh * 8 + x * 2 + 1 - c)
    pending = []

    def chip(k, sign):
        return ((yh + k // 4) % 2) * 4 + (x + sign * (k % 4) + 4) % 4

    def start(copy):
        copy.start()
        pending.append(copy)

    barrier = pltpu.get_barrier_semaphore()
    for i in range(2):
        pl.semaphore_signal(barrier, inc=1, device_id=group_place(i)[0], device_id_type=MESH)
        pl.semaphore_signal(barrier, inc=1, device_id=frame_place(i)[0], device_id_type=MESH)
    for k in NEAR[::-1]:
        pl.semaphore_signal(barrier, inc=1, device_id=(frame, chip(k, 1) * 2 + c), device_id_type=MESH)
    pl.semaphore_signal(barrier, inc=1, device_id=sibling, device_id_type=MESH)

    loads = [
        pltpu.make_async_copy(src, dst, in_s.at[i])
        for i, (src, dst) in enumerate((
            (lat_hbm, lat_ref), (mod_hbm, mod_ref), (sqkv_hbm, qkv0), (so_hbm, wo0), (gate_hbm, gate_ref),
            (bias_hbm, bias_ref), (tqkv_hbm, qkv1), (to_hbm, wo1),
        ))
    ]
    for load in loads:
        load.start()

    def own_rows(core):
        return pl.ds(pl.multiple_of((yh * 4 + x) * 64 + core * TOK, TOK), TOK)

    def rows_of(k, sign, core):
        return pl.ds(pl.multiple_of(chip(k, sign) * 64 + core * TOK, TOK), TOK)

    def send_tokens(st, xb):
        rows = own_rows(c)
        for k in NEAR:
            start(remote(xb.at[rows], xb.at[rows], ag_s.at[st, k], ag_r.at[st, k], (frame, chip(k, 1) * 2 + c)))
        start(remote(xb.at[rows], xb.at[rows], sib_s.at[st, 0], sib_r.at[st, 0], sibling))

    def gather_tokens(st, xb):
        for k in NEAR:
            rows = rows_of(k, -1, c)
            remote(xb.at[rows], xb.at[rows], ag_s.at[st, k], ag_r.at[st, k], sibling).wait_recv()
            start(remote(xb.at[rows], xb.at[rows], sib_s.at[st, k], sib_r.at[st, k], sibling))
        for k in (0,) + NEAR:
            rows = rows_of(k, -1, 1 - c)
            remote(xb.at[rows], xb.at[rows], sib_s.at[st, k], sib_r.at[st, k], sibling).wait_recv()

    def prepare(wm, qkv_ref, wp, wo_ref):
        for m in range(3):
            wm[m * PAD + 64 : (m + 1) * PAD, :] = jnp.zeros((64, D), jnp.bfloat16)
            wm[m * PAD : m * PAD + HD, :] = qkv_ref[m]
        wp[64:, :] = jnp.zeros((64, D), jnp.bfloat16)
        wp[:HD, :] = wo_ref[...]

    def attend(xb, wm, ob, same_position):
        proj = lax.dot_general(
            xb[...], wm[...], (((1,), (1,)), ((), ())), preferred_element_type=jnp.float32
        )
        queries = proj[:, :PAD].astype(jnp.bfloat16)
        keys = proj[:, PAD : 2 * PAD].astype(jnp.bfloat16)
        lane = lax.broadcasted_iota(jnp.int32, (TOTAL, PAD), 1)
        values = jnp.where(lane == HD, 1.0, proj[:, 2 * PAD :]).astype(jnp.bfloat16)
        block = 128
        for i in range(TOTAL // block):
            scores = lax.dot_general(
                queries[i * block : (i + 1) * block], keys, (((1,), (1,)), ((), ())),
                preferred_element_type=jnp.float32,
            )
            if same_position:
                row = lax.broadcasted_iota(jnp.int32, (block, TOTAL), 0)
                col = lax.broadcasted_iota(jnp.int32, (block, TOTAL), 1)
                scores = jnp.where(((row - col) & 15) == 0, scores, -1e30)
            largest = jnp.max(scores, axis=-1, keepdims=True)
            weights = jnp.exp2((scores - largest) * SCALE2).astype(jnp.bfloat16)
            summed = jnp.dot(weights, values, preferred_element_type=jnp.float32)
            done = (summed / summed[:, HD : HD + 1]).astype(jnp.bfloat16)
            ob[i * 2 : (i + 1) * 2] = done.reshape(2, 2, TOK, PAD)

    def project(st, ob, wp, ub, vb, tb, rb):
        weight = wp[...]
        theirs = ob[:, pl.ds(1 - c, 1)].reshape(TOTAL // 2, PAD)
        ub[...] = jnp.dot(theirs, weight, preferred_element_type=jnp.float32).astype(jnp.bfloat16).reshape(8, TOK, D)
        for k in FAR + (0,):
            to = chip(k, 1)
            start(remote(ub.at[to], vb.at[to], u_s.at[st, k], u_r.at[st, k], sibling))
        ours = ob[:, pl.ds(c, 1)].reshape(TOTAL // 2, PAD)
        acc[...] = jnp.dot(ours, weight, preferred_element_type=jnp.float32).reshape(8, TOK, D)
        for k in FAR:
            to = chip(k, 1)
            remote(ub.at[to], vb.at[to], u_s.at[st, k], u_r.at[st, k], sibling).wait_recv()
            tb[k] = (acc[to] + vb[to].astype(jnp.float32)).astype(jnp.bfloat16)
            start(remote(tb.at[k], rb.at[k], t_s.at[st, k], t_r.at[st, k], (frame, to * 2 + c)))
        here = chip(0, 1)
        remote(ub.at[here], vb.at[here], u_s.at[st, 0], u_r.at[st, 0], sibling).wait_recv()
        branch = acc[here] + vb[here].astype(jnp.float32)
        for k in NEAR:
            remote(tb.at[k], rb.at[k], t_s.at[st, k], t_r.at[st, k], sibling).wait_recv()
            branch = branch + rb[k].astype(jnp.float32)
        return gate_ref[st : st + 1, :] * (branch + bias_ref[st : st + 1, :])

    def finish():
        out_ref[...] = jnp.zeros_like(out_ref)
        for load in loads[2:] if len(pending) == 0 else ():
            load.wait()
        for copy in pending:
            copy.wait_send()

    loads[0].wait()
    loads[1].wait()
    latents = lat_ref[0].astype(jnp.float32)
    x0[own_rows(c), :] = normalize(latents, mod_ref[0:1, :], mod_ref[1:2, :])
    pl.semaphore_wait(barrier, len(NEAR) + 1 + 4)
    send_tokens(0, x0)
    for load in loads[2:]:
        load.wait()
    prepare(wm0, qkv0, wp0, wo0)
    gather_tokens(0, x0)
    attend(x0, wm0, o0, False)
    y0[...] = (latents + project(0, o0, wp0, u0, v0, t0, r0)).astype(jnp.bfloat16)

    for i in range(2):
        device, slot = group_place(i)
        start(remote(y0.at[i * 16 : i * 16 + 16], p0.at[slot], p_s.at[0, i], p_r.at[0, slot], device))
    prepare(wm1, qkv1, wp1, wo1)
    for i in range(2):
        remote(p0.at[i], p0.at[i], p_s.at[0, i], p_r.at[0, i], sibling).wait_recv()

    section = p0[...].reshape(TOK, D).astype(jnp.float32)
    x1[own_rows(c), :] = normalize(section, mod_ref[2:3, :], mod_ref[3:4, :])
    send_tokens(1, x1)
    gather_tokens(1, x1)
    attend(x1, wm1, o1, True)
    y1[...] = (section + project(1, o1, wp1, u1, v1, t1, r1)).astype(jnp.bfloat16)

    for i in range(2):
        device, half = frame_place(i)
        start(remote(y1.at[i * 16 : i * 16 + 16], p1.at[half], p_s.at[1, i], p_r.at[1, half], device))
    for i in range(2):
        remote(p1.at[i], p1.at[i], p_s.at[1, i], p_r.at[1, i], sibling).wait_recv()
    out_ref[...] = p1[...].reshape(1, TOK, D)
    for copy in pending:
        copy.wait_send()


def local(latents, spatial_qkv, spatial_out, temporal_qkv, temporal_out, modulation, gates, out_bias):
    bf16, f32, vmem, dma = jnp.bfloat16, jnp.float32, pltpu.VMEM, pltpu.SemaphoreType.DMA
    return pl.pallas_call(
        kernel,
        out_shape=jax.ShapeDtypeStruct(latents.shape, bf16),
        in_specs=[pl.BlockSpec(memory_space=pl.ANY)] * 8,
        out_specs=pl.BlockSpec(memory_space=pltpu.VMEM),
        scratch_shapes=[
            vmem((1, TOK, D), bf16), vmem((3, HD, D), bf16), vmem((3, HD, D), bf16),
            vmem((HD, D), bf16), vmem((HD, D), bf16),
            vmem((4, D), f32), vmem((2, D), f32), vmem((2, D), f32),
            vmem((TOTAL, D), bf16), vmem((TOTAL, D), bf16),
            vmem((3 * PAD, D), bf16), vmem((3 * PAD, D), bf16),
            vmem((PAD, D), bf16), vmem((PAD, D), bf16),
            vmem((8, 2, TOK, PAD), bf16), vmem((8, 2, TOK, PAD), bf16),
            vmem((8, TOK, D), bf16), vmem((8, TOK, D), bf16),
            vmem((8, TOK, D), bf16), vmem((8, TOK, D), bf16),
            vmem((8, TOK, D), bf16), vmem((8, TOK, D), bf16),
            vmem((8, TOK, D), bf16), vmem((8, TOK, D), bf16),
            vmem((8, TOK, D), f32),
            vmem((TOK, D), bf16), vmem((TOK, D), bf16),
            vmem((2, TOK // 2, D), bf16), vmem((2, TOK // 2, D), bf16),
            dma((8,)), dma((2, 8)), dma((2, 8)), dma((2, 8)), dma((2, 8)),
            dma((2, 8)), dma((2, 8)), dma((2, 8)), dma((2, 8)), dma((2, 2)), dma((2, 2)),
        ],
        compiler_params=pltpu.CompilerParams(
            collective_id=0, has_side_effects=True, vmem_limit_bytes=60 << 20
        ),
        name="block_pair",
    )(latents, spatial_qkv, spatial_out, temporal_qkv, temporal_out, modulation, gates, out_bias)


def solution(mesh):
    return jax.shard_map(
        local,
        mesh=mesh,
        in_specs=(
            P("frame", "head", None),
            P(None, "head", None),
            P("head", None),
            P(None, "head", None),
            P("head", None),
            P(),
            P(),
            P(),
        ),
        out_specs=P("frame", "head", None),
        check_vma=False,
    )
```

```python
import jax
import jax.numpy as jnp
from jax import lax
from jax.experimental import pallas as pl
from jax.experimental.pallas import tpu as pltpu
from jax.sharding import PartitionSpec as P

HD = 72
PAD = 128
ROWS = 80
D = 1152
TOK = 32
HALF = TOK // 2
TOTAL = 512
ORDER = (0, 1, 3, 4, 2, 5, 7, 6)
SCALE2 = HD**-0.5 * 1.4426950408889634
VLIM = 60
MESH = pl.DeviceIdType.MESH


def normalize(values, shift_row, scale_row):
    centre = jnp.mean(values, axis=-1, keepdims=True)
    offsets = values - centre
    spread = jnp.mean(offsets * offsets, axis=-1, keepdims=True)
    return (offsets * lax.rsqrt(spread + 1e-6) * (1.0 + scale_row) + shift_row).astype(jnp.bfloat16)


def places():
    frame, head = lax.axis_index("frame"), lax.axis_index("head")
    return frame // 2, frame % 2, head // 8, (head // 2) % 4, head % 2


def group_place(half):
    z, yl, yh, x, c = places()
    zg = c * 8 + half * 4 + x
    turn = (z - zg + 25) % 16
    return (zg * 2 + yh, yl * 8 + ((x + turn // 4) % 4) * 2 + (turn // 2) % 2), turn % 2


def frame_place(slot):
    z, yl, yh, x, c = places()
    turn = ((x - z % 4 + 4) % 4) * 4 + c * 2 + slot
    zf = (z + turn + 7) % 16
    return (zf * 2 + yh, yl * 8 + (z % 4) * 2 + z // 8), (z // 4) % 2


def remote(src, dst, send, recv, device):
    return pltpu.make_async_remote_copy(
        src_ref=src, dst_ref=dst, send_sem=send, recv_sem=recv, device_id=device, device_id_type=MESH
    )


def kernel(
    lat_hbm, sqkv_hbm, so_hbm, tqkv_hbm, to_hbm, mod_hbm, gate_hbm, bias_hbm,
    out_ref,
    lat_ref, qkv0, qkv1, wo0, wo1, mod_ref, gate_ref, bias_ref,
    x0, x1, wm0, wm1, ws0, ws1, wr0, wr1, wp0, wp1, f0, f1, g0, g1,
    u0, u1, v0, v1, t0, t1, r0, r1, acc, y0, y1, p0,
    in_s, ag_s, ag_r, w_s, w_r, q_s, q_r, u_s, u_r, t_s, t_r, p_s, p_r,
):
    frame = lax.axis_index("frame")
    z, yl, yh, x, c = places()
    sibling = (frame, yh * 8 + x * 2 + 1 - c)
    pending = []

    loads = [
        pltpu.make_async_copy(src, dst, in_s.at[i])
        for i, (src, dst) in enumerate((
            (lat_hbm, lat_ref), (mod_hbm, mod_ref), (sqkv_hbm, qkv0), (so_hbm, wo0), (gate_hbm, gate_ref),
            (bias_hbm, bias_ref), (tqkv_hbm, qkv1), (to_hbm, wo1),
        ))
    ]
    for load in loads:
        load.start()

    def chip(i, sign):
        k = ORDER[i]
        return (frame, ((yh + k // 4) % 2) * 8 + ((x + sign * (k % 4) + 4) % 4) * 2 + c)

    def start(copy):
        copy.start()
        pending.append(copy)

    barrier = pltpu.get_barrier_semaphore()
    for i in range(2):
        pl.semaphore_signal(barrier, inc=1, device_id=group_place(i)[0], device_id_type=MESH)
        pl.semaphore_signal(barrier, inc=1, device_id=frame_place(i)[0], device_id_type=MESH)
    for i in range(7, 0, -1):
        pl.semaphore_signal(barrier, inc=1, device_id=chip(i, 1), device_id_type=MESH)
    pl.semaphore_signal(barrier, inc=1, device_id=sibling, device_id_type=MESH)

    def send_tokens(st, half, xb):
        for i in range(7, 0, -1):
            start(remote(xb.at[half, 0], xb.at[half, i], ag_s.at[st, half, i], ag_r.at[st, half, i], chip(i, 1)))

    def transpose_weights(wm, first, rows_ref):
        for m in range(3):
            rows = rows_ref[m * ROWS : (m + 1) * ROWS, :]
            rows = jnp.concatenate([rows, jnp.zeros((PAD - ROWS, D), jnp.bfloat16)], axis=0)
            wm[:, (first + m) * PAD : (first + m + 1) * PAD] = rows.T

    def prepare(st, wm, qkv_ref, ws, wr, wp, wo_ref):
        for m in range(3):
            ws[m * ROWS + 64 : (m + 1) * ROWS, :] = jnp.zeros((16, D), jnp.bfloat16)
            ws[m * ROWS : m * ROWS + HD, :] = qkv_ref[m]
        start(remote(ws, wr, w_s.at[st], w_r.at[st], sibling))
        transpose_weights(wm, 0, ws)
        wp[64:, :] = jnp.zeros((64, D), jnp.bfloat16)
        wp[:HD, :] = wo_ref[...]

    def finish_prepare(st, wm, ws, wr):
        remote(ws, wr, w_s.at[st], w_r.at[st], sibling).wait_recv()
        transpose_weights(wm, 3, wr)

    def project_tokens(st, xb, wm, fb, gb):
        for half in range(2):
            for i in range(1, 8):
                remote(
                    xb.at[half, i], xb.at[half, i], ag_s.at[st, half, i], ag_r.at[st, half, i], sibling
                ).wait_recv()
            proj = jnp.dot(xb[half].reshape(8 * HALF, D), wm[...], preferred_element_type=jnp.float32)
            lane = lax.broadcasted_iota(jnp.int32, proj.shape, 1)
            proj = jnp.where((lane == 2 * PAD + HD) | (lane == 5 * PAD + HD), 1.0, proj)
            proj = proj.astype(jnp.bfloat16).reshape(8, HALF, 6 * PAD)
            gb[half] = proj[:, :, 3 * PAD :]
            start(remote(gb.at[half], fb.at[c, half], q_s.at[st, half], q_r.at[st, half], sibling))
            fb[pl.ds(c, 1), half] = proj[:, :, : 3 * PAD].reshape(1, 8, HALF, 3 * PAD)
        for half in range(2):
            remote(gb.at[half], fb.at[1 - c, half], q_s.at[st, half], q_r.at[st, half], sibling).wait_recv()

    def attend(fb, core, half, same_position):
        keys = fb[:, :, :, :, PAD : 2 * PAD].reshape(TOTAL, PAD)
        values = fb[:, :, :, :, 2 * PAD :].reshape(TOTAL, PAD)
        block = 8 * HALF
        queries = fb[pl.ds(core, 1), half, :, :, :PAD].reshape(block, PAD)
        scores = lax.dot_general(queries, keys, (((1,), (1,)), ((), ())), preferred_element_type=jnp.float32)
        if same_position:
            row = lax.broadcasted_iota(jnp.int32, (block, TOTAL), 0)
            col = lax.broadcasted_iota(jnp.int32, (block, TOTAL), 1)
            scores = jnp.where(((row - col) & 15) == 0, scores, -1e30)
        largest = jnp.max(scores, axis=-1, keepdims=True)
        weights = jnp.exp2((scores - largest) * SCALE2).astype(jnp.bfloat16)
        summed = jnp.dot(weights, values, preferred_element_type=jnp.float32)
        return (summed / summed[:, HD : HD + 1]).astype(jnp.bfloat16)

    def attend_and_project(st, fb, wp, ub, vb, tb, rb, same_position):
        def theirs(half):
            share = jnp.dot(attend(fb, 1 - c, half, same_position), wp[...], preferred_element_type=jnp.float32)
            ub[half] = share.astype(jnp.bfloat16).reshape(8, HALF, D)
            start(remote(ub.at[half], vb.at[half], u_s.at[st, half], u_r.at[st, half], sibling))

        def ours(half):
            share = jnp.dot(attend(fb, c, half, same_position), wp[...], preferred_element_type=jnp.float32)
            acc[half] = share.reshape(8, HALF, D)

        def send_sums(half):
            remote(ub.at[half], vb.at[half], u_s.at[st, half], u_r.at[st, half], sibling).wait_recv()
            for i in range(7, 0, -1):
                tb[half, i] = (acc[half, i] + vb[half, i].astype(jnp.float32)).astype(jnp.bfloat16)
                start(remote(
                    tb.at[half, i], rb.at[half, i], t_s.at[st, half, i], t_r.at[st, half, i], chip(i, -1)
                ))

        theirs(0)
        ours(0)
        theirs(1)
        send_sums(0)
        ours(1)
        send_sums(1)

    def collect(st, half, vb, tb, rb):
        branch = acc[half, 0] + vb[half, 0].astype(jnp.float32)
        for i in range(1, 8):
            remote(
                tb.at[half, i], rb.at[half, i], t_s.at[st, half, i], t_r.at[st, half, i], sibling
            ).wait_recv()
            branch = branch + rb[half, i].astype(jnp.float32)
        return gate_ref[st : st + 1, :] * (branch + bias_ref[st : st + 1, :])

    loads[0].wait()
    loads[1].wait()
    ready = normalize(lat_ref[0].astype(jnp.float32), mod_ref[0:1, :], mod_ref[1:2, :])
    x0[0, 0] = ready[:HALF]
    x0[1, 0] = ready[HALF:]
    pl.semaphore_wait(barrier, 7 + 1 + 4)
    send_tokens(0, 0, x0)
    for load in loads[2:]:
        load.wait()
    prepare(0, wm0, qkv0, ws0, wr0, wp0, wo0)
    send_tokens(0, 1, x0)
    finish_prepare(0, wm0, ws0, wr0)
    project_tokens(0, x0, wm0, f0, g0)
    attend_and_project(0, f0, wp0, u0, v0, t0, r0, False)

    for half in range(2):
        rows = lat_ref[0, half * HALF : (half + 1) * HALF].astype(jnp.float32)
        y0[half] = (rows + collect(0, half, v0, t0, r0)).astype(jnp.bfloat16)
        device, slot = group_place(half)
        start(remote(y0.at[half], p0.at[slot], p_s.at[0, half], p_r.at[0, slot], device))
    prepare(1, wm1, qkv1, ws1, wr1, wp1, wo1)
    finish_prepare(1, wm1, ws1, wr1)

    for slot in range(2):
        remote(p0.at[slot], p0.at[slot], p_s.at[0, slot], p_r.at[0, slot], sibling).wait_recv()
        x1[slot, 0] = normalize(p0[slot].astype(jnp.float32), mod_ref[2:3, :], mod_ref[3:4, :])
        send_tokens(1, slot, x1)
    project_tokens(1, x1, wm1, f1, g1)
    attend_and_project(1, f1, wp1, u1, v1, t1, r1, True)

    for slot in range(2):
        y1[slot] = (p0[slot].astype(jnp.float32) + collect(1, slot, v1, t1, r1)).astype(jnp.bfloat16)
        device, half = frame_place(slot)
        rows = pl.ds(pl.multiple_of(half * HALF, HALF), HALF)
        start(remote(y1.at[slot], out_ref.at[0, rows], p_s.at[1, slot], p_r.at[1, half], device))
    for half in range(2):
        rows = out_ref.at[0, half * HALF : (half + 1) * HALF]
        remote(rows, rows, p_s.at[1, half], p_r.at[1, half], sibling).wait_recv()
    for copy in pending:
        copy.wait_send()


def local(latents, spatial_qkv, spatial_out, temporal_qkv, temporal_out, modulation, gates, out_bias):
    bf16, f32, vmem, dma = jnp.bfloat16, jnp.float32, pltpu.VMEM, pltpu.SemaphoreType.DMA

    def pair(*shape):
        return [vmem(shape, bf16), vmem(shape, bf16)]

    return pl.pallas_call(
        kernel,
        out_shape=jax.ShapeDtypeStruct(latents.shape, bf16),
        in_specs=[pl.BlockSpec(memory_space=pl.ANY)] * 8,
        out_specs=pl.BlockSpec(memory_space=pl.ANY),
        scratch_shapes=[
            vmem((1, TOK, D), bf16), *pair(3, HD, D), *pair(HD, D),
            vmem((4, D), f32), vmem((2, D), f32), vmem((2, D), f32),
            *pair(2, 8, HALF, D), *pair(D, 6 * PAD), *pair(3 * ROWS, D), *pair(3 * ROWS, D), *pair(PAD, D),
            *pair(2, 2, 8, HALF, 3 * PAD), *pair(2, 8, HALF, 3 * PAD),
            *pair(2, 8, HALF, D), *pair(2, 8, HALF, D), *pair(2, 8, HALF, D), *pair(2, 8, HALF, D),
            vmem((2, 8, HALF, D), f32),
            *pair(2, HALF, D), vmem((2, HALF, D), bf16),
            dma((8,)), dma((2, 2, 8)), dma((2, 2, 8)), dma((2,)), dma((2,)), dma((2, 2)), dma((2, 2)),
            dma((2, 2)), dma((2, 2)), dma((2, 2, 8)), dma((2, 2, 8)), dma((2, 2)), dma((2, 2)),
        ],
        compiler_params=pltpu.CompilerParams(
            collective_id=0, has_side_effects=True, vmem_limit_bytes=VLIM << 20
        ),
        name="block_pair",
    )(latents, spatial_qkv, spatial_out, temporal_qkv, temporal_out, modulation, gates, out_bias)


def solution(mesh):
    return jax.shard_map(
        local,
        mesh=mesh,
        in_specs=(
            P("frame", "head", None),
            P(None, "head", None),
            P("head", None),
            P(None, "head", None),
            P("head", None),
            P(),
            P(),
            P(),
        ),
        out_specs=P("frame", "head", None),
        check_vma=False,
    )
```

```python
import jax
import jax.numpy as jnp
from jax import lax
from jax.experimental import pallas as pl
from jax.experimental.pallas import tpu as pltpu
from jax.sharding import PartitionSpec as P

HD = 72
PAD = 128
ROWS = 80
D = 1152
TOK = 32
HALF = TOK // 2
TOTAL = 512
ORDER = (0, 1, 3, 4, 2, 5, 7, 6)
SCALE2 = HD**-0.5 * 1.4426950408889634
VLIM = 60
MESH = pl.DeviceIdType.MESH


def normalize(values, shift_row, scale_row):
    centre = jnp.mean(values, axis=-1, keepdims=True)
    offsets = values - centre
    spread = jnp.mean(offsets * offsets, axis=-1, keepdims=True)
    return (offsets * lax.rsqrt(spread + 1e-6) * (1.0 + scale_row) + shift_row).astype(jnp.bfloat16)


def places():
    frame, head = lax.axis_index("frame"), lax.axis_index("head")
    return frame // 2, frame % 2, head // 8, (head // 2) % 4, head % 2


def group_place(half):
    z, yl, yh, x, c = places()
    zg = c * 8 + half * 4 + x
    turn = (z - zg + 25) % 16
    return (zg * 2 + yh, yl * 8 + ((x + turn // 4) % 4) * 2 + (turn // 2) % 2), turn % 2


def frame_place(slot):
    z, yl, yh, x, c = places()
    turn = ((x - z % 4 + 4) % 4) * 4 + c * 2 + slot
    zf = (z + turn + 7) % 16
    return (zf * 2 + yh, yl * 8 + (z % 4) * 2 + z // 8), (z // 4) % 2


def remote(src, dst, send, recv, device):
    return pltpu.make_async_remote_copy(
        src_ref=src, dst_ref=dst, send_sem=send, recv_sem=recv, device_id=device, device_id_type=MESH
    )


def kernel(
    lat_hbm, sqkv_hbm, so_hbm, tqkv_hbm, to_hbm, mod_hbm, gate_hbm, bias_hbm,
    out_ref,
    lat_ref, qkv0, qkv1, wo0, wo1, mod_ref, gate_ref, bias_ref,
    x0, x1, wm0, wm1, ws0, ws1, wr0, wr1, wp0, wp1, f0, f1, g0, g1,
    u0, u1, v0, v1, t0, t1, r0, r1, acc, y0, y1, p0,
    in_s, ag_s, ag_r, w_s, w_r, q_s, q_r, u_s, u_r, t_s, t_r, p_s, p_r, near_s,
):
    frame = lax.axis_index("frame")
    z, yl, yh, x, c = places()
    sibling = (frame, yh * 8 + x * 2 + 1 - c)
    pending = []

    loads = [
        pltpu.make_async_copy(src, dst, in_s.at[i])
        for i, (src, dst) in enumerate((
            (lat_hbm, lat_ref), (mod_hbm, mod_ref), (sqkv_hbm, qkv0), (so_hbm, wo0), (gate_hbm, gate_ref),
            (bias_hbm, bias_ref), (tqkv_hbm, qkv1), (to_hbm, wo1),
        ))
    ]
    for load in loads:
        load.start()

    def chip(i, sign):
        k = ORDER[i]
        return (frame, ((yh + k // 4) % 2) * 8 + ((x + sign * (k % 4) + 4) % 4) * 2 + c)

    def start(copy):
        copy.start()
        pending.append(copy)

    def signal(sem, device):
        pl.semaphore_signal(sem, inc=1, device_id=device, device_id_type=MESH)

    def signal_along_z(sem, step):
        head = yh * 8 + x * 2 + c
        signal(sem, (((z + step) % 16) * 2 + yl, head))
        signal(sem, (((z + 16 - step) % 16) * 2 + yl, head))

    barrier = pltpu.get_barrier_semaphore()
    other_frame = (z * 2 + 1 - yl, yh * 8 + x * 2 + c)
    for i in range(7, 0, -1):
        signal(barrier, chip(i, 1))
    signal_along_z(barrier, 1)
    signal(barrier, other_frame)
    signal(barrier, sibling)

    def send_tokens(st, half, xb):
        for i in range(7, 0, -1):
            start(remote(xb.at[half, 0], xb.at[half, i], ag_s.at[st, half, i], ag_r.at[st, half, i], chip(i, 1)))

    def transpose_weights(wm, first, rows_ref):
        for m in range(3):
            rows = rows_ref[m * ROWS : (m + 1) * ROWS, :]
            rows = jnp.concatenate([rows, jnp.zeros((PAD - ROWS, D), jnp.bfloat16)], axis=0)
            wm[:, (first + m) * PAD : (first + m + 1) * PAD] = rows.T

    def prepare(st, wm, qkv_ref, ws, wr, wp, wo_ref):
        for m in range(3):
            ws[m * ROWS + 64 : (m + 1) * ROWS, :] = jnp.zeros((16, D), jnp.bfloat16)
            ws[m * ROWS : m * ROWS + HD, :] = qkv_ref[m]
        start(remote(ws, wr, w_s.at[st], w_r.at[st], sibling))
        transpose_weights(wm, 0, ws)
        wp[64:, :] = jnp.zeros((64, D), jnp.bfloat16)
        wp[:HD, :] = wo_ref[...]

    def finish_prepare(st, wm, ws, wr):
        remote(ws, wr, w_s.at[st], w_r.at[st], sibling).wait_recv()
        transpose_weights(wm, 3, wr)

    def project_tokens(st, half, xb, wm, fb, gb):
        for i in range(1, 8):
            remote(
                xb.at[half, i], xb.at[half, i], ag_s.at[st, half, i], ag_r.at[st, half, i], sibling
            ).wait_recv()
        proj = jnp.dot(xb[half].reshape(8 * HALF, D), wm[...], preferred_element_type=jnp.float32)
        lane = lax.broadcasted_iota(jnp.int32, proj.shape, 1)
        proj = jnp.where((lane == 2 * PAD + HD) | (lane == 5 * PAD + HD), 1.0, proj)
        proj = proj.astype(jnp.bfloat16).reshape(8, HALF, 6 * PAD)
        gb[half] = proj[:, :, 3 * PAD :]
        start(remote(gb.at[half], fb.at[c, half], q_s.at[st, half], q_r.at[st, half], sibling))
        fb[pl.ds(c, 1), half] = proj[:, :, : 3 * PAD].reshape(1, 8, HALF, 3 * PAD)

    def swap_tokens(st, fb, gb):
        for half in range(2):
            remote(gb.at[half], fb.at[1 - c, half], q_s.at[st, half], q_r.at[st, half], sibling).wait_recv()

    def attend(fb, core, half, same_position):
        keys = fb[:, :, :, :, PAD : 2 * PAD].reshape(TOTAL, PAD)
        values = fb[:, :, :, :, 2 * PAD :].reshape(TOTAL, PAD)
        block = 8 * HALF
        queries = fb[pl.ds(core, 1), half, :, :, :PAD].reshape(block, PAD)
        scores = lax.dot_general(queries, keys, (((1,), (1,)), ((), ())), preferred_element_type=jnp.float32)
        if same_position:
            row = lax.broadcasted_iota(jnp.int32, (block, TOTAL), 0)
            col = lax.broadcasted_iota(jnp.int32, (block, TOTAL), 1)
            scores = jnp.where(((row - col) & 15) == 0, scores, -1e30)
        largest = jnp.max(scores, axis=-1, keepdims=True)
        weights = jnp.exp2((scores - largest) * SCALE2).astype(jnp.bfloat16)
        summed = jnp.dot(weights, values, preferred_element_type=jnp.float32)
        return (summed / summed[:, HD : HD + 1]).astype(jnp.bfloat16)

    def attend_and_project(st, fb, wp, ub, vb, tb, rb, same_position):
        def theirs(half):
            share = jnp.dot(attend(fb, 1 - c, half, same_position), wp[...], preferred_element_type=jnp.float32)
            ub[half] = share.astype(jnp.bfloat16).reshape(8, HALF, D)
            if st == 0 and half == 0:
                pl.semaphore_wait(near_s.at[3], 1)
            start(remote(ub.at[half], vb.at[half], u_s.at[st, half], u_r.at[st, half], sibling))

        def ours(half):
            share = jnp.dot(attend(fb, c, half, same_position), wp[...], preferred_element_type=jnp.float32)
            acc[half] = share.reshape(8, HALF, D)

        def send_sums(half):
            remote(ub.at[half], vb.at[half], u_s.at[st, half], u_r.at[st, half], sibling).wait_recv()
            for i in range(7, 0, -1):
                tb[half, i] = (acc[half, i] + vb[half, i].astype(jnp.float32)).astype(jnp.bfloat16)
                start(remote(
                    tb.at[half, i], rb.at[half, i], t_s.at[st, half, i], t_r.at[st, half, i], chip(i, -1)
                ))

        theirs(0)
        ours(0)
        theirs(1)
        send_sums(0)
        ours(1)
        send_sums(1)

    def collect(st, half, vb, tb, rb):
        branch = acc[half, 0] + vb[half, 0].astype(jnp.float32)
        for i in range(1, 8):
            remote(
                tb.at[half, i], rb.at[half, i], t_s.at[st, half, i], t_r.at[st, half, i], sibling
            ).wait_recv()
            branch = branch + rb[half, i].astype(jnp.float32)
        return gate_ref[st : st + 1, :] * (branch + bias_ref[st : st + 1, :])

    loads[0].wait()
    loads[1].wait()
    ready = normalize(lat_ref[0].astype(jnp.float32), mod_ref[0:1, :], mod_ref[1:2, :])
    x0[0, 0] = ready[:HALF]
    x0[1, 0] = ready[HALF:]
    pl.semaphore_wait(barrier, 7 + 2 + 1 + 1)
    send_tokens(0, 0, x0)
    signal_along_z(near_s.at[0], 1)
    for load in loads[2:]:
        load.wait()
    prepare(0, wm0, qkv0, ws0, wr0, wp0, wo0)
    send_tokens(0, 1, x0)
    pl.semaphore_wait(near_s.at[0], 2)
    signal_along_z(near_s.at[1], 2)
    finish_prepare(0, wm0, ws0, wr0)
    pl.semaphore_wait(near_s.at[1], 2)
    signal_along_z(near_s.at[2], 4)
    project_tokens(0, 0, x0, wm0, f0, g0)
    project_tokens(0, 1, x0, wm0, f0, g0)
    pl.semaphore_wait(near_s.at[2], 2)
    signal(near_s.at[3], other_frame)
    swap_tokens(0, f0, g0)
    attend_and_project(0, f0, wp0, u0, v0, t0, r0, False)

    for half in range(2):
        rows = lat_ref[0, half * HALF : (half + 1) * HALF].astype(jnp.float32)
        y0[half] = (rows + collect(0, half, v0, t0, r0)).astype(jnp.bfloat16)
        device, slot = group_place(half)
        start(remote(y0.at[half], p0.at[slot], p_s.at[0, half], p_r.at[0, slot], device))
    prepare(1, wm1, qkv1, ws1, wr1, wp1, wo1)
    finish_prepare(1, wm1, ws1, wr1)

    for slot in range(2):
        remote(p0.at[slot], p0.at[slot], p_s.at[0, slot], p_r.at[0, slot], sibling).wait_recv()
        x1[slot, 0] = normalize(p0[slot].astype(jnp.float32), mod_ref[2:3, :], mod_ref[3:4, :])
        send_tokens(1, slot, x1)
    for half in range(2):
        project_tokens(1, half, x1, wm1, f1, g1)
    swap_tokens(1, f1, g1)
    attend_and_project(1, f1, wp1, u1, v1, t1, r1, True)

    for slot in range(2):
        y1[slot] = (p0[slot].astype(jnp.float32) + collect(1, slot, v1, t1, r1)).astype(jnp.bfloat16)
        device, half = frame_place(slot)
        rows = pl.ds(pl.multiple_of(half * HALF, HALF), HALF)
        start(remote(y1.at[slot], out_ref.at[0, rows], p_s.at[1, slot], p_r.at[1, half], device))
    for half in range(2):
        rows = out_ref.at[0, half * HALF : (half + 1) * HALF]
        remote(rows, rows, p_s.at[1, half], p_r.at[1, half], sibling).wait_recv()
    for copy in pending:
        copy.wait_send()


def local(latents, spatial_qkv, spatial_out, temporal_qkv, temporal_out, modulation, gates, out_bias):
    bf16, f32, vmem, dma = jnp.bfloat16, jnp.float32, pltpu.VMEM, pltpu.SemaphoreType.DMA

    def pair(*shape):
        return [vmem(shape, bf16), vmem(shape, bf16)]

    return pl.pallas_call(
        kernel,
        out_shape=jax.ShapeDtypeStruct(latents.shape, bf16),
        in_specs=[pl.BlockSpec(memory_space=pl.ANY)] * 8,
        out_specs=pl.BlockSpec(memory_space=pl.ANY),
        scratch_shapes=[
            vmem((1, TOK, D), bf16), *pair(3, HD, D), *pair(HD, D),
            vmem((4, D), f32), vmem((2, D), f32), vmem((2, D), f32),
            *pair(2, 8, HALF, D), *pair(D, 6 * PAD), *pair(3 * ROWS, D), *pair(3 * ROWS, D), *pair(PAD, D),
            *pair(2, 2, 8, HALF, 3 * PAD), *pair(2, 8, HALF, 3 * PAD),
            *pair(2, 8, HALF, D), *pair(2, 8, HALF, D), *pair(2, 8, HALF, D), *pair(2, 8, HALF, D),
            vmem((2, 8, HALF, D), f32),
            *pair(2, HALF, D), vmem((2, HALF, D), bf16),
            dma((8,)), dma((2, 2, 8)), dma((2, 2, 8)), dma((2,)), dma((2,)), dma((2, 2)), dma((2, 2)),
            dma((2, 2)), dma((2, 2)), dma((2, 2, 8)), dma((2, 2, 8)), dma((2, 2)), dma((2, 2)),
            pltpu.SemaphoreType.REGULAR((4,)),
        ],
        compiler_params=pltpu.CompilerParams(
            collective_id=0, has_side_effects=True, vmem_limit_bytes=VLIM << 20
        ),
        name="block_pair",
    )(latents, spatial_qkv, spatial_out, temporal_qkv, temporal_out, modulation, gates, out_bias)


def solution(mesh):
    return jax.shard_map(
        local,
        mesh=mesh,
        in_specs=(
            P("frame", "head", None),
            P(None, "head", None),
            P("head", None),
            P(None, "head", None),
            P("head", None),
            P(),
            P(),
            P(),
        ),
        out_specs=P("frame", "head", None),
        check_vma=False,
    )
```

```python
import jax
import jax.numpy as jnp
from jax import lax
from jax.experimental import pallas as pl
from jax.experimental.pallas import tpu as pltpu
from jax.sharding import PartitionSpec as P

HD = 72
PAD = 128
ROWS = 80
D = 1152
TOK = 32
HALF = TOK // 2
TOTAL = 512
ORDER = (0, 1, 3, 4, 2, 5, 7, 6)
SCALE2 = HD**-0.5 * 1.4426950408889634
VLIM = 60
MESH = pl.DeviceIdType.MESH


def normalize(values, shift_row, scale_row):
    centre = jnp.mean(values, axis=-1, keepdims=True)
    offsets = values - centre
    spread = jnp.mean(offsets * offsets, axis=-1, keepdims=True)
    return (offsets * lax.rsqrt(spread + 1e-6) * (1.0 + scale_row) + shift_row).astype(jnp.bfloat16)


def places():
    frame, head = lax.axis_index("frame"), lax.axis_index("head")
    return frame // 2, frame % 2, head // 8, (head // 2) % 4, head % 2


def group_place(half):
    z, yl, yh, x, c = places()
    zg = c * 8 + half * 4 + x
    turn = (z - zg + 25) % 16
    return (zg * 2 + yh, yl * 8 + ((x + turn // 4) % 4) * 2 + (turn // 2) % 2), turn % 2


def frame_place(slot):
    z, yl, yh, x, c = places()
    turn = ((x - z % 4 + 4) % 4) * 4 + c * 2 + slot
    zf = (z + turn + 7) % 16
    return (zf * 2 + yh, yl * 8 + (z % 4) * 2 + z // 8), (z // 4) % 2


def remote(src, dst, send, recv, device):
    return pltpu.make_async_remote_copy(
        src_ref=src, dst_ref=dst, send_sem=send, recv_sem=recv, device_id=device, device_id_type=MESH
    )


def kernel(
    lat_hbm, sqkv_hbm, so_hbm, tqkv_hbm, to_hbm, mod_hbm, gate_hbm, bias_hbm,
    out_ref,
    lat_ref, qkv0, qkv1, wo0, wo1, mod_ref, gate_ref, bias_ref,
    x0, x1, wm0, wm1, ws0, ws1, wr0, wr1, wp0, wp1, f0, f1, g0, g1,
    u0, u1, v0, v1, t0, t1, r0, r1, acc, y0, y1, p0,
    in_s, ag_s, ag_r, w_s, w_r, q_s, q_r, u_s, u_r, t_s, t_r, p_s, p_r, near_s,
):
    frame = lax.axis_index("frame")
    z, yl, yh, x, c = places()
    sibling = (frame, yh * 8 + x * 2 + 1 - c)
    pending = []

    loads = [
        pltpu.make_async_copy(src, dst, in_s.at[i])
        for i, (src, dst) in enumerate((
            (lat_hbm, lat_ref), (mod_hbm, mod_ref), (sqkv_hbm, qkv0), (so_hbm, wo0), (gate_hbm, gate_ref),
            (bias_hbm, bias_ref), (tqkv_hbm, qkv1), (to_hbm, wo1),
        ))
    ]
    for load in loads:
        load.start()

    def chip(i, sign):
        k = ORDER[i]
        return (frame, ((yh + k // 4) % 2) * 8 + ((x + sign * (k % 4) + 4) % 4) * 2 + c)

    def start(copy):
        copy.start()
        pending.append(copy)

    def signal(sem, device):
        pl.semaphore_signal(sem, inc=1, device_id=device, device_id_type=MESH)

    def signal_along_z(sem, step):
        head = yh * 8 + x * 2 + c
        signal(sem, (((z + step) % 16) * 2 + yl, head))
        signal(sem, (((z + 16 - step) % 16) * 2 + yl, head))

    def drain(count):
        for copy in pending[:count]:
            copy.wait_send()
        del pending[:count]

    barrier = pltpu.get_barrier_semaphore()
    other_frame = (z * 2 + 1 - yl, yh * 8 + x * 2 + c)
    for i in range(7, 0, -1):
        signal(barrier, chip(i, 1))
    signal_along_z(barrier, 1)
    signal(barrier, other_frame)
    signal(barrier, sibling)

    def send_tokens(st, half, xb):
        for i in range(7, 0, -1):
            start(remote(xb.at[half, 0], xb.at[half, i], ag_s.at[st, half, i], ag_r.at[st, half, i], chip(i, 1)))

    def transpose_weights(wm, first, rows_ref):
        for m in range(3):
            rows = rows_ref[m * ROWS : (m + 1) * ROWS, :]
            rows = jnp.concatenate([rows, jnp.zeros((PAD - ROWS, D), jnp.bfloat16)], axis=0)
            wm[:, (first + m) * PAD : (first + m + 1) * PAD] = rows.T

    def prepare(st, wm, qkv_ref, ws, wr, wp, wo_ref):
        for m in range(3):
            ws[m * ROWS + 64 : (m + 1) * ROWS, :] = jnp.zeros((16, D), jnp.bfloat16)
            ws[m * ROWS : m * ROWS + HD, :] = qkv_ref[m]
        start(remote(ws, wr, w_s.at[st], w_r.at[st], sibling))
        transpose_weights(wm, 0, ws)
        wp[64:, :] = jnp.zeros((64, D), jnp.bfloat16)
        wp[:HD, :] = wo_ref[...]

    def finish_prepare(st, wm, ws, wr):
        remote(ws, wr, w_s.at[st], w_r.at[st], sibling).wait_recv()
        transpose_weights(wm, 3, wr)

    def project_tokens(st, half, xb, wm, fb, gb):
        for i in range(1, 8):
            remote(
                xb.at[half, i], xb.at[half, i], ag_s.at[st, half, i], ag_r.at[st, half, i], sibling
            ).wait_recv()
        tokens = xb[half].reshape(8 * HALF, D)
        lane = lax.broadcasted_iota(jnp.int32, (8 * HALF, 3 * PAD), 1)

        def project(columns):
            proj = jnp.dot(tokens, wm[:, columns], preferred_element_type=jnp.float32)
            return jnp.where(lane == 2 * PAD + HD, 1.0, proj).astype(jnp.bfloat16).reshape(8, HALF, 3 * PAD)

        gb[half] = project(slice(3 * PAD, 6 * PAD))
        start(remote(gb.at[half], fb.at[c, half], q_s.at[st, half], q_r.at[st, half], sibling))
        fb[pl.ds(c, 1), half] = project(slice(0, 3 * PAD)).reshape(1, 8, HALF, 3 * PAD)

    def swap_tokens(st, fb, gb):
        for half in range(2):
            remote(gb.at[half], fb.at[1 - c, half], q_s.at[st, half], q_r.at[st, half], sibling).wait_recv()

    def attend(fb, core, half, same_position):
        keys = fb[:, :, :, :, PAD : 2 * PAD].reshape(TOTAL, PAD)
        values = fb[:, :, :, :, 2 * PAD :].reshape(TOTAL, PAD)
        block = 8 * HALF
        queries = fb[pl.ds(core, 1), half, :, :, :PAD].reshape(block, PAD)
        scores = lax.dot_general(queries, keys, (((1,), (1,)), ((), ())), preferred_element_type=jnp.float32)
        if same_position:
            row = lax.broadcasted_iota(jnp.int32, (block, TOTAL), 0)
            col = lax.broadcasted_iota(jnp.int32, (block, TOTAL), 1)
            scores = jnp.where(((row - col) & 15) == 0, scores, -1e30)
        largest = jnp.max(scores, axis=-1, keepdims=True)
        weights = jnp.exp2((scores - largest) * SCALE2).astype(jnp.bfloat16)
        summed = jnp.dot(weights, values, preferred_element_type=jnp.float32)
        return (summed / summed[:, HD : HD + 1]).astype(jnp.bfloat16)

    def attend_and_project(st, fb, wp, ub, vb, tb, rb, same_position):
        def theirs(half):
            share = jnp.dot(attend(fb, 1 - c, half, same_position), wp[...], preferred_element_type=jnp.float32)
            ub[half] = share.astype(jnp.bfloat16).reshape(8, HALF, D)
            if st == 0 and half == 0:
                pl.semaphore_wait(near_s.at[3], 1)
            for part in (1, 0):
                span = slice(4 * part, 4 * part + 4)
                start(remote(
                    ub.at[half, span], vb.at[half, span], u_s.at[st, half, part], u_r.at[st, half, part], sibling
                ))

        def ours(half):
            share = jnp.dot(attend(fb, c, half, same_position), wp[...], preferred_element_type=jnp.float32)
            acc[half] = share.reshape(8, HALF, D)

        def send_sums(half):
            for part in (1, 0):
                span = slice(4 * part, 4 * part + 4)
                remote(
                    ub.at[half, span], vb.at[half, span], u_s.at[st, half, part], u_r.at[st, half, part], sibling
                ).wait_recv()
                for i in range(4 * part + 3, max(4 * part, 1) - 1, -1):
                    tb[half, i] = (acc[half, i] + vb[half, i].astype(jnp.float32)).astype(jnp.bfloat16)
                    start(remote(
                        tb.at[half, i], rb.at[half, i], t_s.at[st, half, i], t_r.at[st, half, i], chip(i, -1)
                    ))

        theirs(0)
        ours(0)
        send_sums(0)
        theirs(1)
        ours(1)
        send_sums(1)

    def collect(st, half, vb, tb, rb):
        branch = acc[half, 0] + vb[half, 0].astype(jnp.float32)
        for i in range(1, 8):
            remote(
                tb.at[half, i], rb.at[half, i], t_s.at[st, half, i], t_r.at[st, half, i], sibling
            ).wait_recv()
            branch = branch + rb[half, i].astype(jnp.float32)
        return gate_ref[st : st + 1, :] * (branch + bias_ref[st : st + 1, :])

    loads[0].wait()
    loads[1].wait()
    ready = normalize(lat_ref[0].astype(jnp.float32), mod_ref[0:1, :], mod_ref[1:2, :])
    x0[0, 0] = ready[:HALF]
    x0[1, 0] = ready[HALF:]
    pl.semaphore_wait(barrier, 7 + 2 + 1 + 1)
    send_tokens(0, 0, x0)
    send_tokens(0, 1, x0)
    signal_along_z(near_s.at[0], 1)
    for load in loads[2:]:
        load.wait()
    prepare(0, wm0, qkv0, ws0, wr0, wp0, wo0)
    pl.semaphore_wait(near_s.at[0], 2)
    signal_along_z(near_s.at[1], 2)
    finish_prepare(0, wm0, ws0, wr0)
    pl.semaphore_wait(near_s.at[1], 2)
    signal_along_z(near_s.at[2], 4)
    project_tokens(0, 0, x0, wm0, f0, g0)
    project_tokens(0, 1, x0, wm0, f0, g0)
    pl.semaphore_wait(near_s.at[2], 2)
    signal(near_s.at[3], other_frame)
    swap_tokens(0, f0, g0)
    attend_and_project(0, f0, wp0, u0, v0, t0, r0, False)

    sent = len(pending)
    for half in range(2):
        rows = lat_ref[0, half * HALF : (half + 1) * HALF].astype(jnp.float32)
        y0[half] = (rows + collect(0, half, v0, t0, r0)).astype(jnp.bfloat16)
        device, slot = group_place(half)
        start(remote(y0.at[half], p0.at[slot], p_s.at[0, half], p_r.at[0, slot], device))
    prepare(1, wm1, qkv1, ws1, wr1, wp1, wo1)
    drain(sent)
    finish_prepare(1, wm1, ws1, wr1)

    for slot in range(2):
        remote(p0.at[slot], p0.at[slot], p_s.at[0, slot], p_r.at[0, slot], sibling).wait_recv()
        x1[slot, 0] = normalize(p0[slot].astype(jnp.float32), mod_ref[2:3, :], mod_ref[3:4, :])
        send_tokens(1, slot, x1)
    for half in range(2):
        project_tokens(1, half, x1, wm1, f1, g1)
    swap_tokens(1, f1, g1)
    attend_and_project(1, f1, wp1, u1, v1, t1, r1, True)

    sent = len(pending)
    for slot in range(2):
        y1[slot] = (p0[slot].astype(jnp.float32) + collect(1, slot, v1, t1, r1)).astype(jnp.bfloat16)
        device, half = frame_place(slot)
        rows = pl.ds(pl.multiple_of(half * HALF, HALF), HALF)
        start(remote(y1.at[slot], out_ref.at[0, rows], p_s.at[1, slot], p_r.at[1, half], device))
    drain(sent)
    for half in range(2):
        rows = out_ref.at[0, half * HALF : (half + 1) * HALF]
        remote(rows, rows, p_s.at[1, half], p_r.at[1, half], sibling).wait_recv()
    drain(len(pending))


def local(latents, spatial_qkv, spatial_out, temporal_qkv, temporal_out, modulation, gates, out_bias):
    bf16, f32, vmem, dma = jnp.bfloat16, jnp.float32, pltpu.VMEM, pltpu.SemaphoreType.DMA

    def pair(*shape):
        return [vmem(shape, bf16), vmem(shape, bf16)]

    return pl.pallas_call(
        kernel,
        out_shape=jax.ShapeDtypeStruct(latents.shape, bf16),
        in_specs=[pl.BlockSpec(memory_space=pl.ANY)] * 8,
        out_specs=pl.BlockSpec(memory_space=pl.ANY),
        scratch_shapes=[
            vmem((1, TOK, D), bf16), *pair(3, HD, D), *pair(HD, D),
            vmem((4, D), f32), vmem((2, D), f32), vmem((2, D), f32),
            *pair(2, 8, HALF, D), *pair(D, 6 * PAD), *pair(3 * ROWS, D), *pair(3 * ROWS, D), *pair(PAD, D),
            *pair(2, 2, 8, HALF, 3 * PAD), *pair(2, 8, HALF, 3 * PAD),
            *pair(2, 8, HALF, D), *pair(2, 8, HALF, D), *pair(2, 8, HALF, D), *pair(2, 8, HALF, D),
            vmem((2, 8, HALF, D), f32),
            *pair(2, HALF, D), vmem((2, HALF, D), bf16),
            dma((8,)), dma((2, 2, 8)), dma((2, 2, 8)), dma((2,)), dma((2,)), dma((2, 2)), dma((2, 2)),
            dma((2, 2, 2)), dma((2, 2, 2)), dma((2, 2, 8)), dma((2, 2, 8)), dma((2, 2)), dma((2, 2)),
            pltpu.SemaphoreType.REGULAR((4,)),
        ],
        compiler_params=pltpu.CompilerParams(
            collective_id=0, has_side_effects=True, vmem_limit_bytes=VLIM << 20
        ),
        name="block_pair",
    )(latents, spatial_qkv, spatial_out, temporal_qkv, temporal_out, modulation, gates, out_bias)


def solution(mesh):
    return jax.shard_map(
        local,
        mesh=mesh,
        in_specs=(
            P("frame", "head", None),
            P(None, "head", None),
            P("head", None),
            P(None, "head", None),
            P("head", None),
            P(),
            P(),
            P(),
        ),
        out_specs=P("frame", "head", None),
        check_vma=False,
    )
```

```python
import jax
import jax.numpy as jnp
from jax import lax
from jax.experimental import pallas as pl
from jax.experimental.pallas import tpu as pltpu
from jax.sharding import PartitionSpec as P

HD = 72
PAD = 128
ROWS = 80
D = 1152
TOK = 32
HALF = TOK // 2
TOTAL = 512
ORDER = (0, 1, 3, 4, 2, 5, 7, 6)
SCALE2 = HD**-0.5 * 1.4426950408889634
VLIM = 60
MESH = pl.DeviceIdType.MESH


def normalize(values, shift_row, scale_row):
    centre = jnp.mean(values, axis=-1, keepdims=True)
    offsets = values - centre
    spread = jnp.mean(offsets * offsets, axis=-1, keepdims=True)
    return (offsets * lax.rsqrt(spread + 1e-6) * (1.0 + scale_row) + shift_row).astype(jnp.bfloat16)


def places():
    frame, head = lax.axis_index("frame"), lax.axis_index("head")
    return frame // 2, frame % 2, head // 8, (head // 2) % 4, head % 2


def group_place(half):
    z, yl, yh, x, c = places()
    zg = c * 8 + half * 4 + x
    turn = (z - zg + 25) % 16
    return (zg * 2 + yh, yl * 8 + ((x + turn // 4) % 4) * 2 + (turn // 2) % 2), turn % 2


def frame_place(slot):
    z, yl, yh, x, c = places()
    turn = ((x - z % 4 + 4) % 4) * 4 + c * 2 + slot
    zf = (z + turn + 7) % 16
    return (zf * 2 + yh, yl * 8 + (z % 4) * 2 + z // 8), (z // 4) % 2


def remote(src, dst, send, recv, device):
    return pltpu.make_async_remote_copy(
        src_ref=src, dst_ref=dst, send_sem=send, recv_sem=recv, device_id=device, device_id_type=MESH
    )


def kernel(
    lat_hbm, sqkv_hbm, so_hbm, tqkv_hbm, to_hbm, mod_hbm, gate_hbm, bias_hbm,
    out_ref,
    lat_ref, qkv0, qkv1, wo0, wo1, mod_ref, gate_ref, bias_ref,
    x0, x1, wm0, wm1, ws0, ws1, wr0, wr1, wp0, wp1, f0, f1, g0, g1,
    u0, u1, v0, v1, t0, t1, r0, r1, acc, y0, y1, p0,
    in_s, ag_s, ag_r, w_s, w_r, q_s, q_r, u_s, u_r, t_s, t_r, p_s, p_r, near_s,
):
    frame = lax.axis_index("frame")
    z, yl, yh, x, c = places()
    sibling = (frame, yh * 8 + x * 2 + 1 - c)
    pending = []

    loads = [
        pltpu.make_async_copy(src, dst, in_s.at[i])
        for i, (src, dst) in enumerate((
            (lat_hbm, lat_ref), (mod_hbm, mod_ref), (sqkv_hbm, qkv0), (so_hbm, wo0), (gate_hbm, gate_ref),
            (bias_hbm, bias_ref), (tqkv_hbm, qkv1), (to_hbm, wo1),
        ))
    ]
    for load in loads[:2]:
        load.start()

    def chip(i, sign):
        k = ORDER[i]
        return (frame, ((yh + k // 4) % 2) * 8 + ((x + sign * (k % 4) + 4) % 4) * 2 + c)

    def start(copy):
        copy.start()
        pending.append(copy)

    def signal(sem, device):
        pl.semaphore_signal(sem, inc=1, device_id=device, device_id_type=MESH)

    def signal_along_z(sem, step):
        head = yh * 8 + x * 2 + c
        signal(sem, (((z + step) % 16) * 2 + yl, head))
        signal(sem, (((z + 16 - step) % 16) * 2 + yl, head))

    def drain(count):
        for copy in pending[:count]:
            copy.wait_send()
        del pending[:count]

    barrier = pltpu.get_barrier_semaphore()
    other_frame = (z * 2 + 1 - yl, yh * 8 + x * 2 + c)
    for i in range(7, 0, -1):
        signal(barrier, chip(i, 1))
    signal_along_z(barrier, 1)
    signal(barrier, other_frame)
    signal(barrier, sibling)
    for load in loads[2:]:
        load.start()

    def send_tokens(st, half, xb):
        for i in range(7, 0, -1):
            start(remote(xb.at[half, 0], xb.at[half, i], ag_s.at[st, half, i], ag_r.at[st, half, i], chip(i, 1)))

    def transpose_weights(wm, first, rows_ref):
        for m in range(3):
            rows = rows_ref[m * ROWS : (m + 1) * ROWS, :]
            rows = jnp.concatenate([rows, jnp.zeros((PAD - ROWS, D), jnp.bfloat16)], axis=0)
            wm[:, (first + m) * PAD : (first + m + 1) * PAD] = rows.T

    def prepare(st, wm, qkv_ref, ws, wr, wp, wo_ref):
        for m in range(3):
            ws[m * ROWS + 64 : (m + 1) * ROWS, :] = jnp.zeros((16, D), jnp.bfloat16)
            ws[m * ROWS : m * ROWS + HD, :] = qkv_ref[m]
        start(remote(ws, wr, w_s.at[st], w_r.at[st], sibling))
        transpose_weights(wm, 0, ws)
        wp[64:, :] = jnp.zeros((64, D), jnp.bfloat16)
        wp[:HD, :] = wo_ref[...]

    def finish_prepare(st, wm, ws, wr):
        remote(ws, wr, w_s.at[st], w_r.at[st], sibling).wait_recv()
        transpose_weights(wm, 3, wr)

    def project_tokens(st, half, xb, wm, fb, gb):
        for i in range(1, 8):
            remote(
                xb.at[half, i], xb.at[half, i], ag_s.at[st, half, i], ag_r.at[st, half, i], sibling
            ).wait_recv()
        tokens = xb[half].reshape(8 * HALF, D)
        lane = lax.broadcasted_iota(jnp.int32, (8 * HALF, 3 * PAD), 1)

        def project(columns):
            proj = jnp.dot(tokens, wm[:, columns], preferred_element_type=jnp.float32)
            return jnp.where(lane == 2 * PAD + HD, 1.0, proj).astype(jnp.bfloat16).reshape(8, HALF, 3 * PAD)

        gb[half] = project(slice(3 * PAD, 6 * PAD))
        start(remote(gb.at[half], fb.at[c, half], q_s.at[st, half], q_r.at[st, half], sibling))
        fb[pl.ds(c, 1), half] = project(slice(0, 3 * PAD)).reshape(1, 8, HALF, 3 * PAD)

    def swap_tokens(st, fb, gb):
        for half in range(2):
            remote(gb.at[half], fb.at[1 - c, half], q_s.at[st, half], q_r.at[st, half], sibling).wait_recv()

    def attend(fb, core, half, same_position):
        keys = fb[:, :, :, :, PAD : 2 * PAD].reshape(TOTAL, PAD)
        values = fb[:, :, :, :, 2 * PAD :].reshape(TOTAL, PAD)
        block = 8 * HALF
        queries = fb[pl.ds(core, 1), half, :, :, :PAD].reshape(block, PAD)
        scores = lax.dot_general(queries, keys, (((1,), (1,)), ((), ())), preferred_element_type=jnp.float32)
        if same_position:
            row = lax.broadcasted_iota(jnp.int32, (block, TOTAL), 0)
            col = lax.broadcasted_iota(jnp.int32, (block, TOTAL), 1)
            scores = jnp.where(((row - col) & 15) == 0, scores, -1e30)
        largest = jnp.max(scores, axis=-1, keepdims=True)
        weights = jnp.exp2((scores - largest) * SCALE2).astype(jnp.bfloat16)
        summed = jnp.dot(weights, values, preferred_element_type=jnp.float32)
        return (summed / summed[:, HD : HD + 1]).astype(jnp.bfloat16)

    def attend_and_project(st, fb, wp, ub, vb, tb, rb, same_position):
        def theirs(half):
            share = jnp.dot(attend(fb, 1 - c, half, same_position), wp[...], preferred_element_type=jnp.float32)
            ub[half] = share.astype(jnp.bfloat16).reshape(8, HALF, D)
            if st == 0 and half == 0:
                pl.semaphore_wait(near_s.at[3], 1)
            for part in (1, 0):
                span = slice(4 * part, 4 * part + 4)
                start(remote(
                    ub.at[half, span], vb.at[half, span], u_s.at[st, half, part], u_r.at[st, half, part], sibling
                ))

        def ours(half):
            share = jnp.dot(attend(fb, c, half, same_position), wp[...], preferred_element_type=jnp.float32)
            acc[half] = share.reshape(8, HALF, D)

        def send_sums(half):
            for part in (1, 0):
                span = slice(4 * part, 4 * part + 4)
                remote(
                    ub.at[half, span], vb.at[half, span], u_s.at[st, half, part], u_r.at[st, half, part], sibling
                ).wait_recv()
                for i in range(4 * part + 3, max(4 * part, 1) - 1, -1):
                    tb[half, i] = (acc[half, i] + vb[half, i].astype(jnp.float32)).astype(jnp.bfloat16)
                    start(remote(
                        tb.at[half, i], rb.at[half, i], t_s.at[st, half, i], t_r.at[st, half, i], chip(i, -1)
                    ))

        theirs(0)
        ours(0)
        send_sums(0)
        theirs(1)
        ours(1)
        send_sums(1)

    def collect(st, half, vb, tb, rb):
        branch = acc[half, 0] + vb[half, 0].astype(jnp.float32)
        for i in range(1, 8):
            remote(
                tb.at[half, i], rb.at[half, i], t_s.at[st, half, i], t_r.at[st, half, i], sibling
            ).wait_recv()
            branch = branch + rb[half, i].astype(jnp.float32)
        return gate_ref[st : st + 1, :] * (branch + bias_ref[st : st + 1, :])

    loads[0].wait()
    loads[1].wait()
    ready = normalize(lat_ref[0].astype(jnp.float32), mod_ref[0:1, :], mod_ref[1:2, :])
    x0[0, 0] = ready[:HALF]
    x0[1, 0] = ready[HALF:]
    pl.semaphore_wait(barrier, 7 + 2 + 1 + 1)
    send_tokens(0, 0, x0)
    send_tokens(0, 1, x0)
    signal_along_z(near_s.at[0], 1)
    for load in loads[2:]:
        load.wait()
    prepare(0, wm0, qkv0, ws0, wr0, wp0, wo0)
    pl.semaphore_wait(near_s.at[0], 2)
    signal_along_z(near_s.at[1], 2)
    finish_prepare(0, wm0, ws0, wr0)
    pl.semaphore_wait(near_s.at[1], 2)
    signal_along_z(near_s.at[2], 4)
    project_tokens(0, 0, x0, wm0, f0, g0)
    project_tokens(0, 1, x0, wm0, f0, g0)
    pl.semaphore_wait(near_s.at[2], 2)
    signal(near_s.at[3], other_frame)
    swap_tokens(0, f0, g0)
    attend_and_project(0, f0, wp0, u0, v0, t0, r0, False)

    sent = len(pending)
    for half in range(2):
        rows = lat_ref[0, half * HALF : (half + 1) * HALF].astype(jnp.float32)
        y0[half] = (rows + collect(0, half, v0, t0, r0)).astype(jnp.bfloat16)
        device, slot = group_place(half)
        start(remote(y0.at[half], p0.at[slot], p_s.at[0, half], p_r.at[0, slot], device))
    prepare(1, wm1, qkv1, ws1, wr1, wp1, wo1)
    drain(sent)
    finish_prepare(1, wm1, ws1, wr1)

    for slot in range(2):
        remote(p0.at[slot], p0.at[slot], p_s.at[0, slot], p_r.at[0, slot], sibling).wait_recv()
        x1[slot, 0] = normalize(p0[slot].astype(jnp.float32), mod_ref[2:3, :], mod_ref[3:4, :])
        send_tokens(1, slot, x1)
    for half in range(2):
        project_tokens(1, half, x1, wm1, f1, g1)
    swap_tokens(1, f1, g1)
    attend_and_project(1, f1, wp1, u1, v1, t1, r1, True)

    sent = len(pending)
    for slot in range(2):
        y1[slot] = (p0[slot].astype(jnp.float32) + collect(1, slot, v1, t1, r1)).astype(jnp.bfloat16)
        device, half = frame_place(slot)
        rows = pl.ds(pl.multiple_of(half * HALF, HALF), HALF)
        start(remote(y1.at[slot], out_ref.at[0, rows], p_s.at[1, slot], p_r.at[1, half], device))
    drain(sent)
    for half in range(2):
        rows = out_ref.at[0, half * HALF : (half + 1) * HALF]
        remote(rows, rows, p_s.at[1, half], p_r.at[1, half], sibling).wait_recv()
    drain(len(pending))


def local(latents, spatial_qkv, spatial_out, temporal_qkv, temporal_out, modulation, gates, out_bias):
    bf16, f32, vmem, dma = jnp.bfloat16, jnp.float32, pltpu.VMEM, pltpu.SemaphoreType.DMA

    def pair(*shape):
        return [vmem(shape, bf16), vmem(shape, bf16)]

    return pl.pallas_call(
        kernel,
        out_shape=jax.ShapeDtypeStruct(latents.shape, bf16),
        in_specs=[pl.BlockSpec(memory_space=pl.ANY)] * 8,
        out_specs=pl.BlockSpec(memory_space=pl.ANY),
        scratch_shapes=[
            vmem((1, TOK, D), bf16), *pair(3, HD, D), *pair(HD, D),
            vmem((4, D), f32), vmem((2, D), f32), vmem((2, D), f32),
            *pair(2, 8, HALF, D), *pair(D, 6 * PAD), *pair(3 * ROWS, D), *pair(3 * ROWS, D), *pair(PAD, D),
            *pair(2, 2, 8, HALF, 3 * PAD), *pair(2, 8, HALF, 3 * PAD),
            *pair(2, 8, HALF, D), *pair(2, 8, HALF, D), *pair(2, 8, HALF, D), *pair(2, 8, HALF, D),
            vmem((2, 8, HALF, D), f32),
            *pair(2, HALF, D), vmem((2, HALF, D), bf16),
            dma((8,)), dma((2, 2, 8)), dma((2, 2, 8)), dma((2,)), dma((2,)), dma((2, 2)), dma((2, 2)),
            dma((2, 2, 2)), dma((2, 2, 2)), dma((2, 2, 8)), dma((2, 2, 8)), dma((2, 2)), dma((2, 2)),
            pltpu.SemaphoreType.REGULAR((4,)),
        ],
        compiler_params=pltpu.CompilerParams(
            collective_id=0, has_side_effects=True, vmem_limit_bytes=VLIM << 20
        ),
        name="block_pair",
    )(latents, spatial_qkv, spatial_out, temporal_qkv, temporal_out, modulation, gates, out_bias)


def solution(mesh):
    return jax.shard_map(
        local,
        mesh=mesh,
        in_specs=(
            P("frame", "head", None),
            P(None, "head", None),
            P("head", None),
            P(None, "head", None),
            P("head", None),
            P(),
            P(),
            P(),
        ),
        out_specs=P("frame", "head", None),
        check_vma=False,
    )
```
